256 devices in a mesh: seq: 128 (over y, x_lo, z, core), mp: 2 (over x_hi).
Axes of the slice: x: 4 (x_hi: 2, x_lo: 2; x = x_hi * 2 + x_lo), y: 4, z: 8, core: 2. Of those that a mesh axis runs over, the one named last changes fastest.
Arguments:
- norm_gain: float32 [4096], P('mp'), may hold values from 0.25 to 1.75
- queries: bfloat16 [65536, 4096], P('seq', 'mp'), may hold values from -6 to 6
- keys: bfloat16 [65536, 4096], P('seq', 'mp'), may hold values from -6 to 6
- values: bfloat16 [65536, 4096], P('seq', 'mp'), may hold values from -6 to 6
Outputs:
- attended: bfloat16 [65536, 4096], P('seq', 'mp')
The draws below stay inside these ranges and needn't reach their ends.
All inputs are finite; a program needn't handle non-finite values.
Results may differ from the reference program's by a relative error of at most 0.012.
Values may be sent and summed in bfloat16 or wider, within the bound.
A program may use at most 128 MiB of HBM per device.

```python
import math
import jax
import jax.numpy as jnp
from jax import lax

D = 4096
HEADS = 32
HEAD_DIM = 128
TOK_DEV = 512
TOKENS = 65536


def draw_keys(key, part):
    key = jax.random.fold_in(key, 5)
    base = jnp.clip(jax.random.normal(key, (TOKENS, D), jnp.float32), -6.0, 6.0)
    return base.astype(jnp.bfloat16)


def draw_queries(key, part):
    key = jax.random.fold_in(key, 7)
    base = jnp.clip(jax.random.normal(key, (TOKENS, D), jnp.float32), -6.0, 6.0)
    return base.astype(jnp.bfloat16)


def steps_of(own_key, dims, split, smallest, high):
    level = 1.0
    for axis_at, blocks in split:
        heights = jax.random.uniform(jax.random.fold_in(jax.random.fold_in(own_key, 6), axis_at), (blocks,), jnp.float32, smallest / len(split), high / len(split))
        level = level * jnp.repeat(jnp.exp(heights), dims[axis_at] // blocks).reshape((-1,) + (1,) * (len(dims) - 1 - axis_at))
    return level


def scatter_about(stream_key, dims, spread, reach, pieces=(), held_as=jnp.bfloat16):
    gain = steps_of(stream_key, dims, pieces, -0.22, 0.18) if pieces else 1.0
    array = jax.random.normal(stream_key, dims, jnp.float32) * spread * gain
    return jnp.minimum(jnp.maximum(array, -reach), reach).astype(held_as)


def setup_inputs(seed: int = 0) -> dict:
    key_of = jax.random.split(jax.random.key(seed), 5)
    norm_gain = jnp.clip(1.0 + 0.15 * jax.random.normal(key_of[0], (D,), jnp.float32), 0.25, 1.75)
    queries = draw_queries(jax.random.fold_in(key_of[4], 71), 0)
    keys = draw_keys(jax.random.fold_in(key_of[4], 71), 0)
    values = scatter_about(key_of[3], (TOKENS, D), 1.0, 6.0, ((0, 128), (1, 2)))
    return dict(norm_gain=norm_gain, queries=queries, keys=keys, values=values)


def window_mask(row_count, block):
    target = jnp.arange(row_count, dtype=jnp.int32)[:, None]
    source = jnp.arange(4 * row_count, dtype=jnp.int32)[None, :]
    distance = 3 - source // row_count
    offset_in = source % row_count
    return (block >= distance) & ((distance > 0) | (offset_in <= target))

def reference(norm_gain, queries, keys, values):
    block_count = TOKENS // TOK_DEV
    key_pad = jnp.concatenate([jnp.zeros((3 * TOK_DEV, D), jnp.bfloat16), keys], 0)
    value_pad = jnp.concatenate([jnp.zeros((3 * TOK_DEV, D), jnp.bfloat16), values], 0)

    def one_block(block):
        start = block * TOK_DEV
        query_part = lax.dynamic_slice_in_dim(queries, start, TOK_DEV, 0).astype(jnp.float32)
        key_part = lax.dynamic_slice_in_dim(key_pad, start, 4 * TOK_DEV, 0).astype(jnp.float32)
        value_part = lax.dynamic_slice_in_dim(value_pad, start, 4 * TOK_DEV, 0).astype(jnp.float32)
        query_part = query_part.reshape(TOK_DEV, HEADS, HEAD_DIM)
        key_part = key_part.reshape(4 * TOK_DEV, HEADS, HEAD_DIM)
        value_part = value_part.reshape(4 * TOK_DEV, HEADS, HEAD_DIM)
        scores = jnp.einsum('thd,shd->hts', query_part, key_part) / math.sqrt(HEAD_DIM)
        allowed = window_mask(TOK_DEV, block)
        scores = jnp.where(allowed[None], scores, -1e+30)
        weights = jax.nn.softmax(scores, axis=-1).astype(jnp.bfloat16)
        output = jnp.einsum('hts,shd->thd', weights.astype(jnp.float32), value_part)
        heads_out = output.reshape(TOK_DEV, D)
        meansq = lax.optimization_barrier(jnp.mean(heads_out * heads_out, axis=1, keepdims=True))
        return (heads_out * lax.rsqrt(meansq + 1e-06) * norm_gain).astype(jnp.bfloat16)
    stacked = lax.map(one_block, jnp.arange(block_count, dtype=jnp.int32))
    return stacked.reshape(TOKENS, D)
```

```python
import functools
import math

import jax
import jax.numpy as jnp
from jax import lax
from jax.experimental import pallas as pl
from jax.experimental.pallas import tpu as pltpu
from jax.sharding import PartitionSpec as P

D = 4096
HEAD_DIM = 128
MESH = pl.DeviceIdType.MESH
SCALE = math.log2(math.e) / math.sqrt(HEAD_DIM)
EXCLUDED = -1e30

LEAD = 3
FORWARD_1, FORWARD_2, TASK_3, TASK_2, TASK_1, TASK_0 = 0, 1, 2, 3, 4, 5


def partial_attention(keys, values_t, queries, causal):
    scores = lax.dot_general(
        keys, queries, (((1,), (1,)), ((), ())), preferred_element_type=jnp.float32
    )
    if causal:
        rows, tile = scores.shape
        source = lax.broadcasted_iota(jnp.int32, (rows, tile), 0)
        target = lax.broadcasted_iota(jnp.int32, (rows, tile), 1) + (rows - tile)
        scores = jnp.where(source <= target, scores, EXCLUDED)
    top = jnp.max(scores, axis=0, keepdims=True) * SCALE
    weights = jnp.exp2(scores * SCALE - top)
    total = jnp.sum(weights, axis=0, keepdims=True)
    output = lax.dot_general(
        values_t,
        weights.astype(jnp.bfloat16),
        (((1,), (0,)), ((), ())),
        preferred_element_type=jnp.float32,
    )
    return output, top, total


def kernel(
    n, heads, rows,
    gain_ref, q_hbm, k_hbm, v_hbm, out_hbm,
    q_own, k_own, v_own, v_t, q_in, o_in, l_in, o_out, l_out, attended, finished,
    squares, squares_in,
    load_sem, q_send, q_recv, o_send, o_recv, l_send, l_recv, s_send, s_recv, out_sem,
):
    me = lax.axis_index("seq")
    partner = 1 - lax.axis_index("mp")
    left, right = jnp.maximum(me - 1, 0), jnp.minimum(me + 1, n - 1)
    has_left, has_right = me > 0, me < n - 1
    half = rows // 2
    to_left, to_right = {"seq": left}, {"seq": right}

    def columns(h):
        return pl.ds(pl.multiple_of(h * HEAD_DIM, HEAD_DIM), HEAD_DIM)

    def load(which, h):
        source, target = ((q_hbm, q_own), (k_hbm, k_own), (v_hbm, v_own))[which]
        return pltpu.make_async_copy(
            source.at[:, columns(h)], target.at[h], load_sem.at[which, h]
        )

    def send_q(step, h):
        source = q_hbm.at[:, columns(h)] if step == 0 else q_in.at[step - 1, h]
        return pltpu.make_async_remote_copy(
            src_ref=source, dst_ref=q_in.at[step, h],
            send_sem=q_send.at[step, h], recv_sem=q_recv.at[step, h],
            device_id=to_left, device_id_type=MESH,
        )

    def send_o(step, h):
        return pltpu.make_async_remote_copy(
            src_ref=o_out.at[step, h], dst_ref=o_in.at[step, h],
            send_sem=o_send.at[step, h], recv_sem=o_recv.at[step, h],
            device_id=to_right, device_id_type=MESH,
        )

    def send_l(step, h):
        return pltpu.make_async_remote_copy(
            src_ref=l_out.at[step, h], dst_ref=l_in.at[step, h],
            send_sem=l_send.at[step, h], recv_sem=l_recv.at[step, h],
            device_id=to_right, device_id_type=MESH,
        )

    def send_s():
        return pltpu.make_async_remote_copy(
            src_ref=squares, dst_ref=squares_in, send_sem=s_send, recv_sem=s_recv,
            device_id={"mp": partner}, device_id_type=MESH,
        )

    barrier = pltpu.get_barrier_semaphore()

    @pl.when(has_left)
    def _():
        pl.semaphore_signal(barrier, inc=1, device_id=to_left, device_id_type=MESH)

    @pl.when(has_right)
    def _():
        pl.semaphore_signal(barrier, inc=1, device_id=to_right, device_id_type=MESH)

    pl.semaphore_signal(barrier, inc=1, device_id={"mp": partner}, device_id_type=MESH)

    @pl.loop(0, heads)
    def _(h):
        for which in range(3):
            load(which, h).start()

    squares[...] = jnp.zeros_like(squares)

    @pl.when(jnp.logical_not(has_left))
    def _():
        @pl.loop(0, heads)
        def _(h):
            for step in range(3):
                o_in[step, h] = jnp.zeros(o_in.shape[2:], o_in.dtype)
                l_in[step, h] = jnp.full(l_in.shape[2:], EXCLUDED, l_in.dtype)

    pl.semaphore_wait(
        barrier, 1 + has_left.astype(jnp.int32) + has_right.astype(jnp.int32)
    )

    @pl.when(has_left)
    def _():
        for h in range(min(LEAD, heads)):
            send_q(0, h).start()

    def staged(r, skew, distance, run):
        h = r - skew
        @pl.when((h >= 0) & (h < heads) & (me + distance < n))
        def _():
            run(h)

    def prepare(h):
        for which in range(3):
            load(which, h).wait()
        v_t[h] = v_own[h].T

    def forward(step, h):
        send_q(step - 1, h).wait_recv()

        @pl.when(has_left)
        def _():
            send_q(step, h).start()

    def task(distance, h):
        causal = distance == 0
        if distance:
            queries = q_in.at[distance - 1, h]
        else:
            queries = q_own.at[h]
        if distance == 3:
            send_q(2, h).wait_recv()
        parts = []
        for at in range(0, rows, half):
            depth = at + half if causal else rows
            parts.append(
                partial_attention(
                    k_own[h, :depth], v_t[h, :, :depth], queries[at : at + half], causal
                )
            )
        if distance < 3:
            @pl.when(has_left)
            def _():
                send_o(2 - distance, h).wait_recv()
                send_l(2 - distance, h).wait_recv()

        for at, (output, top, total) in zip(range(0, rows, half), parts):
            span = slice(at, at + half)
            if distance == 3:
                mixed = output / total
                level = top + jnp.log2(total)
            else:
                before = l_in[2 - distance, h, :, span]
                high = jnp.maximum(before, top)
                weight_before = jnp.exp2(before - high)
                weight_here = jnp.exp2(top - high)
                whole = weight_before + weight_here * total
                mixed = (
                    o_in[2 - distance, h, :, span].astype(jnp.float32) * (weight_before / whole)
                    + output * (weight_here / whole)
                )
                level = high + jnp.log2(whole)
            if distance:
                o_out[3 - distance, h, :, span] = mixed.astype(jnp.bfloat16)
                l_out[3 - distance, h, :, span] = level
            else:
                attended[h, span] = mixed.T
                squares[:, span] += jnp.sum(mixed * mixed, axis=0, keepdims=True)
        if distance:
            send_o(3 - distance, h).start()
            send_l(3 - distance, h).start()

    @pl.loop(0, heads + TASK_0)
    def _(r):
        @pl.when(has_left & (r + LEAD < heads))
        def _():
            send_q(0, r + LEAD).start()

        staged(r, 0, 0, prepare)
        staged(r, FORWARD_1, 1, functools.partial(forward, 1))
        staged(r, FORWARD_2, 2, functools.partial(forward, 2))
        staged(r, TASK_3, 3, functools.partial(task, 3))
        staged(r, TASK_2, 2, functools.partial(task, 2))
        staged(r, TASK_1, 1, functools.partial(task, 1))
        staged(r, TASK_0, 0, functools.partial(task, 0))

    send_s().start()
    send_s().wait()
    scale = lax.rsqrt((squares[...] + squares_in[...]) / D + 1e-06)
    scale = jnp.broadcast_to(scale, (HEAD_DIM, rows)).T

    def store(h):
        return pltpu.make_async_copy(finished.at[h], out_hbm.at[:, columns(h)], out_sem.at[h])

    @pl.loop(0, heads)
    def _(h):
        gain = gain_ref[h]
        finished[h] = (attended[h] * scale * gain).astype(jnp.bfloat16)
        store(h).start()

    @pl.loop(0, heads)
    def _(h):
        store(h).wait()
        for step in range(3):
            @pl.when(has_left & (me + step < n))
            def _():
                send_q(step, h).wait_send()

            @pl.when(me + 3 - step < n)
            def _():
                send_o(step, h).wait_send()
                send_l(step, h).wait_send()


def solution(mesh):
    n = mesh.shape["seq"]

    def shards(norm_gain, queries, keys, values):
        rows, width = queries.shape
        heads = width // HEAD_DIM
        by_head = (heads, rows, HEAD_DIM)
        turned = (heads, HEAD_DIM, rows)
        dma = pltpu.SemaphoreType.DMA
        gain = norm_gain.reshape(heads, 1, HEAD_DIM)
        return pl.pallas_call(
            functools.partial(kernel, n, heads, rows),
            out_shape=jax.ShapeDtypeStruct(queries.shape, jnp.bfloat16),
            in_specs=[pl.BlockSpec(memory_space=pltpu.VMEM)]
            + [pl.BlockSpec(memory_space=pl.ANY)] * 3,
            out_specs=pl.BlockSpec(memory_space=pl.ANY),
            scratch_shapes=[
                pltpu.VMEM(by_head, jnp.bfloat16),
                pltpu.VMEM(by_head, jnp.bfloat16),
                pltpu.VMEM(by_head, jnp.bfloat16),
                pltpu.VMEM(turned, jnp.bfloat16),
                pltpu.VMEM((3, *by_head), jnp.bfloat16),
                pltpu.VMEM((3, *turned), jnp.bfloat16),
                pltpu.VMEM((3, heads, 1, rows), jnp.float32),
                pltpu.VMEM((3, *turned), jnp.bfloat16),
                pltpu.VMEM((3, heads, 1, rows), jnp.float32),
                pltpu.VMEM(by_head, jnp.float32),
                pltpu.VMEM(by_head, jnp.bfloat16),
                pltpu.VMEM((1, rows), jnp.float32),
                pltpu.VMEM((1, rows), jnp.float32),
                dma((3, heads)),
                dma((3, heads)),
                dma((3, heads)),
                dma((3, heads)),
                dma((3, heads)),
                dma((3, heads)),
                dma((3, heads)),
                dma,
                dma,
                dma((heads,)),
            ],
            compiler_params=pltpu.CompilerParams(
                collective_id=0, has_side_effects=True, vmem_limit_bytes=56 << 20
            ),
            cost_estimate=pl.CostEstimate(
                flops=16 * heads * rows * rows * HEAD_DIM,
                bytes_accessed=8 * rows * width,
                transcendentals=4 * heads * rows * rows,
            ),
        )(gain, queries, keys, values)

    placed = (P("mp"), P("seq", "mp"), P("seq", "mp"), P("seq", "mp"))
    return jax.shard_map(
        shards, mesh=mesh, in_specs=placed, out_specs=P("seq", "mp"), check_vma=False
    )
```

```python
import functools
import math

import jax
import jax.numpy as jnp
from jax import lax
from jax.experimental import pallas as pl
from jax.experimental.pallas import tpu as pltpu
from jax.sharding import PartitionSpec as P

D = 4096
HEAD_DIM = 128
MESH = pl.DeviceIdType.MESH
SCALE = math.log2(math.e) / math.sqrt(HEAD_DIM)
EXCLUDED = -1e30

SHIPPED = 2
LEAD = 2
FORWARD_1, FORWARD_2, ATTEND, MERGE_2, MERGE_1, MERGE_0 = (1, 3), (1, 5), (4, 6), (6, 7), (7, 8), (10, 12)
SHIP_1, SHIP_2, ATTEND_SHIPPED = (2, 2), (4, 5), (6, 7)
SLOTS = max(b - a for a, b in zip(ATTEND, MERGE_0)) + 1
TILE = 128


def across(a, b):
    return lax.dot_general(a, b, (((1,), (1,)), ((), ())), preferred_element_type=jnp.float32)


def lanes_to_row(column):
    return column.T[:1]


def row_to_lanes(row):
    return jnp.broadcast_to(row, (HEAD_DIM, row.shape[1])).T


def kernel(
    n, heads, kept, rows,
    gain_ref, q_hbm, k_hbm, v_hbm, out_hbm,
    q_own, k_own, v_own, q_in, o_in, l_in, o_out, l_out, o_own, l_own, k_in, v_in, attended, finished,
    squares, row_out, row_in,
    load_sem, q_send, q_recv, o_send, o_recv, l_send, l_recv, kv_send, kv_recv, s_send, s_recv, out_sem,
):
    me = lax.axis_index("seq")
    partner = 1 - lax.axis_index("mp")
    left, right = jnp.maximum(me - 1, 0), jnp.minimum(me + 1, n - 1)
    has_left, has_right = me > 0, me < n - 1
    tile = min(TILE, rows)
    to_left, to_right = {"seq": left}, {"seq": right}

    def columns(h):
        return pl.ds(pl.multiple_of(h * HEAD_DIM, HEAD_DIM), HEAD_DIM)

    def load(which, h):
        source, target = ((q_hbm, q_own), (k_hbm, k_own), (v_hbm, v_own))[which]
        return pltpu.make_async_copy(
            source.at[:, columns(h)], target.at[h], load_sem.at[which, h]
        )

    def send_q(step, h):
        source = q_hbm.at[:, columns(h)] if step == 0 else q_in.at[step - 1, h]
        return pltpu.make_async_remote_copy(
            src_ref=source, dst_ref=q_in.at[step, h],
            send_sem=q_send.at[step, h], recv_sem=q_recv.at[step, h],
            device_id=to_left, device_id_type=MESH,
        )

    def send_o(step, h):
        return pltpu.make_async_remote_copy(
            src_ref=o_out.at[step, h], dst_ref=o_in.at[step, h],
            send_sem=o_send.at[step, h], recv_sem=o_recv.at[step, h],
            device_id=to_right, device_id_type=MESH,
        )

    def send_l(step, h):
        return pltpu.make_async_remote_copy(
            src_ref=l_out.at[step, h], dst_ref=l_in.at[step, h],
            send_sem=l_send.at[step, h], recv_sem=l_recv.at[step, h],
            device_id=to_right, device_id_type=MESH,
        )

    def send_kv(which, step, j):
        source, target = ((k_hbm, k_in), (v_hbm, v_in))[which]
        source = target.at[step - 1, j] if step else source.at[:, columns(kept + j)]
        return pltpu.make_async_remote_copy(
            src_ref=source, dst_ref=target.at[step, j],
            send_sem=kv_send.at[which, step, j], recv_sem=kv_recv.at[which, step, j],
            device_id=to_right, device_id_type=MESH,
        )

    def send_s():
        return pltpu.make_async_remote_copy(
            src_ref=row_out, dst_ref=row_in, send_sem=s_send, recv_sem=s_recv,
            device_id={"mp": partner}, device_id_type=MESH,
        )

    barrier = pltpu.get_barrier_semaphore()

    @pl.when(has_left)
    def _():
        pl.semaphore_signal(barrier, inc=1, device_id=to_left, device_id_type=MESH)

    @pl.when(has_right)
    def _():
        pl.semaphore_signal(barrier, inc=1, device_id=to_right, device_id_type=MESH)

    pl.semaphore_signal(barrier, inc=1, device_id={"mp": partner}, device_id_type=MESH)

    @pl.loop(0, heads)
    def _(h):
        for which in range(3):
            load(which, h).start()

    squares[...] = jnp.zeros_like(squares)

    @pl.when(jnp.logical_not(has_left))
    def _():
        @pl.loop(0, kept)
        def _(h):
            for step in range(3):
                o_in[step, h] = jnp.zeros(o_in.shape[2:], o_in.dtype)
                l_in[step, h] = jnp.full(l_in.shape[2:], EXCLUDED, l_in.dtype)

    for step in range(3):
        @pl.when(me <= step)
        def _():
            for j in range(heads - kept):
                k_in[step, j] = jnp.zeros(k_in.shape[2:], k_in.dtype)
                v_in[step, j] = jnp.zeros(v_in.shape[2:], v_in.dtype)

    pl.semaphore_wait(
        barrier, 1 + has_left.astype(jnp.int32) + has_right.astype(jnp.int32)
    )

    @pl.when(has_right)
    def _():
        for j in range(heads - kept):
            for which in range(2):
                send_kv(which, 0, j).start()

    @pl.when(has_left)
    def _():
        for h in range(min(LEAD, kept)):
            send_q(0, h).start()

    def rounds(skew):
        return skew[0] + lax.rem(me, 2) * (skew[1] - skew[0])

    def staged(r, skew, distance, run):
        h = r - rounds(skew)
        @pl.when((h >= 0) & (h < kept) & (me + distance < n))
        def _():
            run(h)

    def staged_shipped(r, skew, run):
        j = r - rounds(skew)
        @pl.when((j >= 0) & (j < heads - kept))
        def _():
            run(j)

    def ship(step, j):
        @pl.when(me >= step)
        def _():
            for which in range(2):
                send_kv(which, step - 1, j).wait_recv()

                @pl.when(has_right)
                def _():
                    send_kv(which, step, j).start()

    def attend_shipped(j):
        h = kept + j
        for which in range(3):
            load(which, h).wait()

        @pl.when(me >= 3)
        def _():
            for which in range(2):
                send_kv(which, 2, j).wait_recv()

        ones = jnp.ones((rows, HEAD_DIM), jnp.bfloat16)
        for at in range(0, rows, tile):
            span = slice(at, at + tile)
            queries = q_own[h, span]
            parts = [causal(across(queries, k_own[h, : at + tile]), at)]
            for step in range(3):
                scores = across(queries, k_in[step, j])
                parts.append(jnp.where(me > step, scores, EXCLUDED))
            top = functools.reduce(
                jnp.maximum, [jnp.max(part, axis=1, keepdims=True) for part in parts]
            )
            both = jnp.zeros((tile, 2 * HEAD_DIM), jnp.float32)
            for step, scores in enumerate(parts):
                weights = jnp.exp2(scores * SCALE - top * SCALE).astype(jnp.bfloat16)
                values = v_in[step - 1, j] if step else v_own[h, : at + tile]
                values = jnp.concatenate([values, ones[: values.shape[0]]], 1)
                both += jnp.dot(weights, values, preferred_element_type=jnp.float32)
            mixed = both[:, :HEAD_DIM] / both[:, HEAD_DIM:]
            attended[h, span] = mixed
            squares[span] += mixed * mixed

    def causal(scores, at):
        target = lax.broadcasted_iota(jnp.int32, scores.shape, 0) + at
        source = lax.broadcasted_iota(jnp.int32, scores.shape, 1)
        return jnp.where(source <= target, scores, EXCLUDED)

    def forward(step, h):
        send_q(step - 1, h).wait_recv()

        @pl.when(has_left)
        def _():
            send_q(step, h).start()

    def attend(h):
        for which in range(3):
            load(which, h).wait()

        @pl.when(me + 3 < n)
        def _():
            send_q(2, h).wait_recv()

        slot = lax.rem(h, SLOTS)
        keys = k_own[h]
        values = jnp.concatenate([v_own[h], jnp.ones((rows, HEAD_DIM), jnp.bfloat16)], 1)
        lane = lax.broadcasted_iota(jnp.int32, (tile, HEAD_DIM), 1)
        for at in range(0, rows, tile):
            span = slice(at, at + tile)
            levels = jnp.zeros((tile, HEAD_DIM), jnp.float32)
            for distance in (3, 2, 1, 0):
                depth = rows if distance else at + tile
                queries = q_in[distance - 1, h, span] if distance else q_own[h, span]
                scores = across(queries, keys[:depth])
                if not distance:
                    scores = causal(scores, at)
                top = jnp.max(scores, axis=1, keepdims=True) * SCALE
                weights = jnp.exp2(scores * SCALE - top).astype(jnp.bfloat16)
                both = jnp.dot(weights, values[:depth], preferred_element_type=jnp.float32)
                total = both[:, HEAD_DIM:]
                output = both[:, :HEAD_DIM] * (1.0 / total)
                levels = jnp.where(lane == distance, top + jnp.log2(total), levels)
                if distance == 3:
                    o_out[0, h, span] = output.astype(jnp.bfloat16)
                else:
                    o_own[slot, distance, span] = output
            turned = levels.T
            l_out[0, h, :, span] = turned[3:4]
            l_own[slot, :, span] = turned[:4]

        @pl.when(me + 3 < n)
        def _():
            send_o(0, h).start()
            send_l(0, h).start()

    def merge(distance, h):
        step = 3 - distance

        @pl.when(has_left)
        def _():
            send_o(step - 1, h).wait_recv()
            send_l(step - 1, h).wait_recv()

        slot = lax.rem(h, SLOTS)
        here, before = l_own[slot, distance : distance + 1], l_in[step - 1, h]
        share = 1.0 / (1.0 + jnp.exp2(here - before))
        if distance:
            gap = -jnp.abs(here - before)
            l_out[step, h] = jnp.maximum(here, before) + jnp.log2(1.0 + jnp.exp2(gap))
        share = row_to_lanes(share)
        mine = o_own[slot, distance]
        mixed = mine + share * (o_in[step - 1, h].astype(jnp.float32) - mine)
        if distance:
            o_out[step, h] = mixed.astype(jnp.bfloat16)
            send_o(step, h).start()
            send_l(step, h).start()
        else:
            attended[h] = mixed
            squares[...] += mixed * mixed

    @pl.loop(0, kept + max(MERGE_0))
    def _(r):
        staged_shipped(r, SHIP_1, functools.partial(ship, 1))
        staged_shipped(r, SHIP_2, functools.partial(ship, 2))
        staged_shipped(r, ATTEND_SHIPPED, attend_shipped)
        staged(r, FORWARD_1, 1, functools.partial(forward, 1))
        staged(r, MERGE_0, 0, functools.partial(merge, 0))

        @pl.when(has_left & (r + LEAD < kept))
        def _():
            send_q(0, r + LEAD).start()

        staged(r, MERGE_2, 2, functools.partial(merge, 2))
        staged(r, ATTEND, 0, attend)
        staged(r, FORWARD_2, 2, functools.partial(forward, 2))
        staged(r, MERGE_1, 1, functools.partial(merge, 1))

    row_out[...] = lanes_to_row(
        jnp.broadcast_to(jnp.sum(squares[...], axis=1, keepdims=True), squares.shape)
    )
    send_s().start()
    send_s().wait()
    scale = row_to_lanes(lax.rsqrt((row_out[...] + row_in[...]) / D + 1e-06))

    def store(h):
        return pltpu.make_async_copy(finished.at[h], out_hbm.at[:, columns(h)], out_sem.at[h])

    @pl.loop(0, heads)
    def _(h):
        gain = gain_ref[h]
        finished[h] = (attended[h] * scale * gain).astype(jnp.bfloat16)
        store(h).start()

    @pl.loop(0, heads)
    def _(h):
        store(h).wait()

    @pl.loop(0, kept)
    def _(h):
        for step in range(3):
            @pl.when(has_left & (me + step < n))
            def _():
                send_q(step, h).wait_send()

            @pl.when(me + 3 - step < n)
            def _():
                send_o(step, h).wait_send()
                send_l(step, h).wait_send()

    for step in range(3):
        @pl.when(has_right & (me >= step))
        def _():
            for j in range(heads - kept):
                for which in range(2):
                    send_kv(which, step, j).wait_send()


def solution(mesh):
    n = mesh.shape["seq"]

    def shards(norm_gain, queries, keys, values):
        rows, width = queries.shape
        heads = width // HEAD_DIM
        kept = heads - SHIPPED
        by_head = (heads, rows, HEAD_DIM)
        moved = (3, kept, rows, HEAD_DIM)
        shipped = (3, SHIPPED, rows, HEAD_DIM)
        dma = pltpu.SemaphoreType.DMA
        gain = norm_gain.reshape(heads, 1, HEAD_DIM)
        return pl.pallas_call(
            functools.partial(kernel, n, heads, kept, rows),
            out_shape=jax.ShapeDtypeStruct(queries.shape, jnp.bfloat16),
            in_specs=[pl.BlockSpec(memory_space=pltpu.VMEM)]
            + [pl.BlockSpec(memory_space=pl.ANY)] * 3,
            out_specs=pl.BlockSpec(memory_space=pl.ANY),
            scratch_shapes=[
                pltpu.VMEM(by_head, jnp.bfloat16),
                pltpu.VMEM(by_head, jnp.bfloat16),
                pltpu.VMEM(by_head, jnp.bfloat16),
                pltpu.VMEM(moved, jnp.bfloat16),
                pltpu.VMEM(moved, jnp.bfloat16),
                pltpu.VMEM((3, kept, 1, rows), jnp.float32),
                pltpu.VMEM(moved, jnp.bfloat16),
                pltpu.VMEM((3, kept, 1, rows), jnp.float32),
                pltpu.VMEM((SLOTS, 3, rows, HEAD_DIM), jnp.float32),
                pltpu.VMEM((SLOTS, 4, rows), jnp.float32),
                pltpu.VMEM(shipped, jnp.bfloat16),
                pltpu.VMEM(shipped, jnp.bfloat16),
                pltpu.VMEM(by_head, jnp.float32),
                pltpu.VMEM(by_head, jnp.bfloat16),
                pltpu.VMEM((rows, HEAD_DIM), jnp.float32),
                pltpu.VMEM((1, rows), jnp.float32),
                pltpu.VMEM((1, rows), jnp.float32),
                dma((3, heads)),
                dma((3, kept)),
                dma((3, kept)),
                dma((3, kept)),
                dma((3, kept)),
                dma((3, kept)),
                dma((3, kept)),
                dma((2, 3, SHIPPED)),
                dma((2, 3, SHIPPED)),
                dma,
                dma,
                dma((heads,)),
            ],
            compiler_params=pltpu.CompilerParams(
                collective_id=0, has_side_effects=True, vmem_limit_bytes=56 << 20
            ),
            cost_estimate=pl.CostEstimate(
                flops=16 * heads * rows * rows * HEAD_DIM,
                bytes_accessed=8 * rows * width,
                transcendentals=4 * heads * rows * rows,
            ),
        )(gain, queries, keys, values)

    placed = (P("mp"), P("seq", "mp"), P("seq", "mp"), P("seq", "mp"))
    return jax.shard_map(
        shards, mesh=mesh, in_specs=placed, out_specs=P("seq", "mp"), check_vma=False
    )
```

```python
import functools
import math

import jax
import jax.numpy as jnp
from jax import lax
from jax.experimental import pallas as pl
from jax.experimental.pallas import tpu as pltpu
from jax.sharding import PartitionSpec as P

D = 4096
HEAD_DIM = 128
MESH = pl.DeviceIdType.MESH
SCALE = math.log2(math.e) / math.sqrt(HEAD_DIM)
EXCLUDED = -1e30

SHIPPED = 2
LEAD = 2
FORWARD_1, FORWARD_2, ATTEND, MERGE_2, MERGE_1, MERGE_0 = (1, 3), (1, 5), (4, 6), (6, 7), (7, 8), (10, 12)
SHIP_1, SHIP_2, ATTEND_SHIPPED = (2, 2), (4, 5), (6, 7)
SLOTS = max(b - a for a, b in zip(ATTEND, MERGE_0)) + 1
TILE = 128


def across(a, b):
    return lax.dot_general(a, b, (((1,), (1,)), ((), ())), preferred_element_type=jnp.float32)


def lanes_to_row(column):
    return column.T[:1]


def row_to_lanes(row):
    return jnp.broadcast_to(row, (HEAD_DIM, row.shape[1])).T


def kernel(
    n, heads, kept, rows,
    q_hbm, k_hbm, v_hbm, attended, scale_ref,
    q_own, k_own, v_own, q_in, o_in, l_in, o_out, l_out, o_own, l_own, k_in, v_in,
    squares, row_out, row_in,
    load_sem, q_send, q_recv, o_send, o_recv, l_send, l_recv, kv_send, kv_recv, s_send, s_recv,
):
    me = lax.axis_index("seq")
    partner = 1 - lax.axis_index("mp")
    left, right = jnp.maximum(me - 1, 0), jnp.minimum(me + 1, n - 1)
    has_left, has_right = me > 0, me < n - 1
    tile = min(TILE, rows)
    to_left, to_right = {"seq": left}, {"seq": right}

    def columns(h):
        return pl.ds(pl.multiple_of(h * HEAD_DIM, HEAD_DIM), HEAD_DIM)

    def load(which, h):
        source, target = ((q_hbm, q_own), (k_hbm, k_own), (v_hbm, v_own))[which]
        return pltpu.make_async_copy(
            source.at[:, columns(h)], target.at[h], load_sem.at[which, h]
        )

    def send_q(step, h):
        source = q_hbm.at[:, columns(h)] if step == 0 else q_in.at[step - 1, h]
        return pltpu.make_async_remote_copy(
            src_ref=source, dst_ref=q_in.at[step, h],
            send_sem=q_send.at[step], recv_sem=q_recv.at[step, h],
            device_id=to_left, device_id_type=MESH,
        )

    def send_o(step, h):
        return pltpu.make_async_remote_copy(
            src_ref=o_out.at[step, h], dst_ref=o_in.at[step, h],
            send_sem=o_send.at[step], recv_sem=o_recv.at[step, h],
            device_id=to_right, device_id_type=MESH,
        )

    def send_l(step, h):
        return pltpu.make_async_remote_copy(
            src_ref=l_out.at[step, h], dst_ref=l_in.at[step, h],
            send_sem=l_send.at[step], recv_sem=l_recv.at[step, h],
            device_id=to_right, device_id_type=MESH,
        )

    def send_kv(which, step, j):
        source, target = ((k_hbm, k_in), (v_hbm, v_in))[which]
        source = target.at[step - 1, j] if step else source.at[:, columns(kept + j)]
        return pltpu.make_async_remote_copy(
            src_ref=source, dst_ref=target.at[step, j],
            send_sem=kv_send.at[which, step], recv_sem=kv_recv.at[which, step, j],
            device_id=to_right, device_id_type=MESH,
        )

    def send_s():
        return pltpu.make_async_remote_copy(
            src_ref=row_out, dst_ref=row_in, send_sem=s_send, recv_sem=s_recv,
            device_id={"mp": partner}, device_id_type=MESH,
        )

    barrier = pltpu.get_barrier_semaphore()

    @pl.when(has_left)
    def _():
        pl.semaphore_signal(barrier, inc=1, device_id=to_left, device_id_type=MESH)

    @pl.when(has_right)
    def _():
        pl.semaphore_signal(barrier, inc=1, device_id=to_right, device_id_type=MESH)

    pl.semaphore_signal(barrier, inc=1, device_id={"mp": partner}, device_id_type=MESH)

    @pl.loop(0, heads)
    def _(h):
        for which in range(3):
            load(which, h).start()

    squares[...] = jnp.zeros_like(squares)

    @pl.when(jnp.logical_not(has_left))
    def _():
        @pl.loop(0, kept)
        def _(h):
            for step in range(3):
                o_in[step, h] = jnp.zeros(o_in.shape[2:], o_in.dtype)
                l_in[step, h] = jnp.full(l_in.shape[2:], EXCLUDED, l_in.dtype)

    for step in range(3):
        @pl.when(me <= step)
        def _():
            for j in range(heads - kept):
                k_in[step, j] = jnp.zeros(k_in.shape[2:], k_in.dtype)
                v_in[step, j] = jnp.zeros(v_in.shape[2:], v_in.dtype)

    pl.semaphore_wait(
        barrier, 1 + has_left.astype(jnp.int32) + has_right.astype(jnp.int32)
    )

    @pl.when(has_right)
    def _():
        for j in range(heads - kept):
            for which in range(2):
                send_kv(which, 0, j).start()

    @pl.when(has_left)
    def _():
        for h in range(min(LEAD, kept)):
            send_q(0, h).start()

    def rounds(skew):
        return skew[0] + lax.rem(me, 2) * (skew[1] - skew[0])

    def staged(r, skew, distance, run):
        h = r - rounds(skew)
        @pl.when((h >= 0) & (h < kept) & (me + distance < n))
        def _():
            run(h)

    def staged_shipped(r, skew, run):
        j = r - rounds(skew)
        @pl.when((j >= 0) & (j < heads - kept))
        def _():
            run(j)

    def ship(step, j):
        @pl.when(me >= step)
        def _():
            for which in range(2):
                send_kv(which, step - 1, j).wait_recv()

                @pl.when(has_right)
                def _():
                    send_kv(which, step, j).start()

    def attend_shipped(j):
        h = kept + j
        for which in range(3):
            load(which, h).wait()

        @pl.when(me >= 3)
        def _():
            for which in range(2):
                send_kv(which, 2, j).wait_recv()

        ones = jnp.ones((rows, HEAD_DIM), jnp.bfloat16)
        for at in range(0, rows, tile):
            span = slice(at, at + tile)
            queries = q_own[h, span]
            parts = [causal(across(queries, k_own[h, : at + tile]), at)]
            for step in range(3):
                scores = across(queries, k_in[step, j])
                parts.append(jnp.where(me > step, scores, EXCLUDED))
            top = functools.reduce(
                jnp.maximum, [jnp.max(part, axis=1, keepdims=True) for part in parts]
            )
            both = jnp.zeros((tile, 2 * HEAD_DIM), jnp.float32)
            for step, scores in enumerate(parts):
                weights = jnp.exp2(scores * SCALE - top * SCALE).astype(jnp.bfloat16)
                values = v_in[step - 1, j] if step else v_own[h, : at + tile]
                values = jnp.concatenate([values, ones[: values.shape[0]]], 1)
                both += jnp.dot(weights, values, preferred_element_type=jnp.float32)
            mixed = both[:, :HEAD_DIM] / both[:, HEAD_DIM:]
            attended[h, span] = mixed
            squares[span] += mixed * mixed

    def causal(scores, at):
        target = lax.broadcasted_iota(jnp.int32, scores.shape, 0) + at
        source = lax.broadcasted_iota(jnp.int32, scores.shape, 1)
        return jnp.where(source <= target, scores, EXCLUDED)

    def forward(step, h):
        send_q(step - 1, h).wait_recv()

        @pl.when(has_left)
        def _():
            send_q(step, h).start()

    def attend(h):
        for which in range(3):
            load(which, h).wait()

        @pl.when(me + 3 < n)
        def _():
            send_q(2, h).wait_recv()

        slot = lax.rem(h, SLOTS)
        keys = k_own[h]
        values = jnp.concatenate([v_own[h], jnp.ones((rows, HEAD_DIM), jnp.bfloat16)], 1)
        lane = lax.broadcasted_iota(jnp.int32, (tile, HEAD_DIM), 1)
        for at in range(0, rows, tile):
            span = slice(at, at + tile)
            levels = jnp.zeros((tile, HEAD_DIM), jnp.float32)
            for distance in (3, 2, 1, 0):
                depth = rows if distance else at + tile
                queries = q_in[distance - 1, h, span] if distance else q_own[h, span]
                scores = across(queries, keys[:depth])
                if not distance:
                    scores = causal(scores, at)
                top = jnp.max(scores, axis=1, keepdims=True) * SCALE
                weights = jnp.exp2(scores * SCALE - top).astype(jnp.bfloat16)
                both = jnp.dot(weights, values[:depth], preferred_element_type=jnp.float32)
                total = both[:, HEAD_DIM:]
                output = both[:, :HEAD_DIM] * (1.0 / total)
                levels = jnp.where(lane == distance, top + jnp.log2(total), levels)
                if distance == 3:
                    o_out[0, h, span] = output.astype(jnp.bfloat16)
                else:
                    o_own[slot, distance, span] = output
            turned = levels.T
            l_out[0, h, :, span] = turned[3:4]
            l_own[slot, :, span] = turned[:4]

        @pl.when(me + 3 < n)
        def _():
            send_o(0, h).start()
            send_l(0, h).start()

    def merge(distance, h):
        step = 3 - distance

        @pl.when(has_left)
        def _():
            send_o(step - 1, h).wait_recv()
            send_l(step - 1, h).wait_recv()

        slot = lax.rem(h, SLOTS)
        here, before = l_own[slot, distance : distance + 1], l_in[step - 1, h]
        share = 1.0 / (1.0 + jnp.exp2(here - before))
        if distance:
            gap = -jnp.abs(here - before)
            l_out[step, h] = jnp.maximum(here, before) + jnp.log2(1.0 + jnp.exp2(gap))
        share = row_to_lanes(share)
        mine = o_own[slot, distance]
        mixed = mine + share * (o_in[step - 1, h].astype(jnp.float32) - mine)
        if distance:
            o_out[step, h] = mixed.astype(jnp.bfloat16)
            send_o(step, h).start()
            send_l(step, h).start()
        else:
            attended[h] = mixed
            squares[...] += mixed * mixed

    @pl.loop(0, kept + max(MERGE_0))
    def _(r):
        staged_shipped(r, SHIP_1, functools.partial(ship, 1))
        staged_shipped(r, SHIP_2, functools.partial(ship, 2))
        staged_shipped(r, ATTEND_SHIPPED, attend_shipped)
        staged(r, FORWARD_1, 1, functools.partial(forward, 1))
        staged(r, MERGE_0, 0, functools.partial(merge, 0))

        @pl.when(has_left & (r + LEAD < kept))
        def _():
            send_q(0, r + LEAD).start()

        staged(r, MERGE_2, 2, functools.partial(merge, 2))
        staged(r, ATTEND, 0, attend)
        staged(r, FORWARD_2, 2, functools.partial(forward, 2))
        staged(r, MERGE_1, 1, functools.partial(merge, 1))

    row_out[...] = lanes_to_row(
        jnp.broadcast_to(jnp.sum(squares[...], axis=1, keepdims=True), squares.shape)
    )
    send_s().start()

    def drain(buffer, sem):
        pltpu.make_async_copy(buffer, buffer, sem).wait()

    for step in range(3):
        @pl.when(has_left & (me + step < n))
        def _():
            drain(q_in.at[step], q_send.at[step])

        @pl.when(me + 3 - step < n)
        def _():
            drain(o_out.at[step], o_send.at[step])
            drain(l_out.at[step], l_send.at[step])

        @pl.when(has_right & (me >= step))
        def _():
            drain(k_in.at[step], kv_send.at[0, step])
            drain(v_in.at[step], kv_send.at[1, step])

    send_s().wait()
    scale_ref[...] = row_to_lanes(lax.rsqrt((row_out[...] + row_in[...]) / D + 1e-06))


def finish(gain_ref, attended, scale_ref, out_hbm, finished, sem):
    heads, rows, _ = attended.shape
    chunk = rows // 4

    def store(i):
        span = pl.ds(i * chunk, chunk)
        return pltpu.make_async_copy(finished.at[span], out_hbm.at[span], sem.at[i])

    for i in range(4):
        span = slice(i * chunk, (i + 1) * chunk)
        for h in range(heads):
            columns = slice(h * HEAD_DIM, (h + 1) * HEAD_DIM)
            scaled = attended[h, span] * scale_ref[span] * gain_ref[h]
            finished[span, columns] = scaled.astype(jnp.bfloat16)
        store(i).start()
    for i in range(4):
        store(i).wait()


def solution(mesh):
    n = mesh.shape["seq"]

    def shards(norm_gain, queries, keys, values):
        rows, width = queries.shape
        heads = width // HEAD_DIM
        kept = heads - SHIPPED
        by_head = (heads, rows, HEAD_DIM)
        moved = (3, kept, rows, HEAD_DIM)
        shipped = (3, SHIPPED, rows, HEAD_DIM)
        dma = pltpu.SemaphoreType.DMA
        gain = norm_gain.reshape(heads, 1, HEAD_DIM)
        whole = pl.BlockSpec(memory_space=pltpu.VMEM)
        attended, scale = pl.pallas_call(
            functools.partial(kernel, n, heads, kept, rows),
            out_shape=[
                pltpu.VMEM(by_head, jnp.float32),
                pltpu.VMEM((rows, HEAD_DIM), jnp.float32),
            ],
            in_specs=[pl.BlockSpec(memory_space=pl.ANY)] * 3,
            out_specs=[whole, whole],
            scratch_shapes=[
                pltpu.VMEM(by_head, jnp.bfloat16),
                pltpu.VMEM(by_head, jnp.bfloat16),
                pltpu.VMEM(by_head, jnp.bfloat16),
                pltpu.VMEM(moved, jnp.bfloat16),
                pltpu.VMEM(moved, jnp.bfloat16),
                pltpu.VMEM((3, kept, 1, rows), jnp.float32),
                pltpu.VMEM(moved, jnp.bfloat16),
                pltpu.VMEM((3, kept, 1, rows), jnp.float32),
                pltpu.VMEM((SLOTS, 3, rows, HEAD_DIM), jnp.float32),
                pltpu.VMEM((SLOTS, 4, rows), jnp.float32),
                pltpu.VMEM(shipped, jnp.bfloat16),
                pltpu.VMEM(shipped, jnp.bfloat16),
                pltpu.VMEM((rows, HEAD_DIM), jnp.float32),
                pltpu.VMEM((1, rows), jnp.float32),
                pltpu.VMEM((1, rows), jnp.float32),
                dma((3, heads)),
                dma((3,)),
                dma((3, kept)),
                dma((3,)),
                dma((3, kept)),
                dma((3,)),
                dma((3, kept)),
                dma((2, 3)),
                dma((2, 3, SHIPPED)),
                dma,
                dma,
            ],
            compiler_params=pltpu.CompilerParams(
                collective_id=0, has_side_effects=True, vmem_limit_bytes=56 << 20
            ),
            cost_estimate=pl.CostEstimate(
                flops=16 * heads * rows * rows * HEAD_DIM,
                bytes_accessed=8 * rows * width,
                transcendentals=4 * heads * rows * rows,
            ),
        )(queries, keys, values)
        return pl.pallas_call(
            finish,
            out_shape=jax.ShapeDtypeStruct(queries.shape, jnp.bfloat16),
            in_specs=[whole] * 3,
            out_specs=pl.BlockSpec(memory_space=pl.ANY),
            scratch_shapes=[pltpu.VMEM((rows, width), jnp.bfloat16), dma((4,))],
            compiler_params=pltpu.CompilerParams(vmem_limit_bytes=16 << 20),
        )(gain, attended, scale)

    placed = (P("mp"), P("seq", "mp"), P("seq", "mp"), P("seq", "mp"))
    return jax.shard_map(
        shards, mesh=mesh, in_specs=placed, out_specs=P("seq", "mp"), check_vma=False
    )
```

```python
import functools
import math

import jax
import jax.numpy as jnp
from jax import lax
from jax.experimental import pallas as pl
from jax.experimental.pallas import tpu as pltpu
from jax.sharding import PartitionSpec as P

D = 4096
HEAD_DIM = 128
MESH = pl.DeviceIdType.MESH
SCALE = math.log2(math.e) / math.sqrt(HEAD_DIM)
EXCLUDED = -1e30

SHIPPED = 2
LEAD = 1
FORWARD_1, FORWARD_2, ATTEND, MERGE_2, MERGE_1, MERGE_0 = (2, 6), (2, 8), (5, 9), (7, 10), (9, 11), (15, 16)
SHIP_1, SHIP_2, ATTEND_SHIPPED = (3, 6), (5, 8), (7, 10)
SLOTS = max(b - a for a, b in zip(ATTEND, MERGE_0)) + 1
TILE = 128


def across(a, b):
    return lax.dot_general(a, b, (((1,), (1,)), ((), ())), preferred_element_type=jnp.float32)


def lanes_to_row(column):
    return column.T[:1]


def row_to_lanes(row):
    return jnp.broadcast_to(row, (HEAD_DIM, row.shape[1])).T


def kernel(
    n, heads, kept, rows,
    q_hbm, k_hbm, v_hbm, attended, scale_ref,
    q_own, k_own, v_own, q_in, o_in, l_in, o_out, l_out, o_own, l_own, k_in, v_in,
    squares, row_out, row_in,
    load_sem, q_send, q_recv, o_send, o_recv, l_send, l_recv, kv_send, kv_recv, s_send, s_recv,
):
    me = lax.axis_index("seq")
    partner = 1 - lax.axis_index("mp")
    left, right = jnp.maximum(me - 1, 0), jnp.minimum(me + 1, n - 1)
    has_left, has_right = me > 0, me < n - 1
    tile = min(TILE, rows)
    to_left, to_right = {"seq": left}, {"seq": right}

    def columns(h):
        return pl.ds(pl.multiple_of(h * HEAD_DIM, HEAD_DIM), HEAD_DIM)

    def load(which, h):
        source, target = ((q_hbm, q_own), (k_hbm, k_own), (v_hbm, v_own))[which]
        return pltpu.make_async_copy(
            source.at[:, columns(h)], target.at[h], load_sem.at[which, h]
        )

    def send_q(step, h):
        source = q_hbm.at[:, columns(h)] if step == 0 else q_in.at[step - 1, h]
        return pltpu.make_async_remote_copy(
            src_ref=source, dst_ref=q_in.at[step, h],
            send_sem=q_send.at[step], recv_sem=q_recv.at[step, h],
            device_id=to_left, device_id_type=MESH,
        )

    def send_o(step, h):
        return pltpu.make_async_remote_copy(
            src_ref=o_out.at[step, h], dst_ref=o_in.at[step, h],
            send_sem=o_send.at[step], recv_sem=o_recv.at[step, h],
            device_id=to_right, device_id_type=MESH,
        )

    def send_l(step, h):
        return pltpu.make_async_remote_copy(
            src_ref=l_out.at[step, h], dst_ref=l_in.at[step, h],
            send_sem=l_send.at[step], recv_sem=l_recv.at[step, h],
            device_id=to_right, device_id_type=MESH,
        )

    def send_kv(which, step, j):
        source, target = ((k_hbm, k_in), (v_hbm, v_in))[which]
        source = target.at[step - 1, j] if step else source.at[:, columns(kept + j)]
        return pltpu.make_async_remote_copy(
            src_ref=source, dst_ref=target.at[step, j],
            send_sem=kv_send.at[which, step], recv_sem=kv_recv.at[which, step, j],
            device_id=to_right, device_id_type=MESH,
        )

    def send_s():
        return pltpu.make_async_remote_copy(
            src_ref=row_out, dst_ref=row_in, send_sem=s_send, recv_sem=s_recv,
            device_id={"mp": partner}, device_id_type=MESH,
        )

    barrier = pltpu.get_barrier_semaphore()

    @pl.when(has_left)
    def _():
        pl.semaphore_signal(barrier, inc=1, device_id=to_left, device_id_type=MESH)

    @pl.when(has_right)
    def _():
        pl.semaphore_signal(barrier, inc=1, device_id=to_right, device_id_type=MESH)

    pl.semaphore_signal(barrier, inc=1, device_id={"mp": partner}, device_id_type=MESH)

    squares[...] = jnp.zeros_like(squares)

    @pl.when(jnp.logical_not(has_left))
    def _():
        @pl.loop(0, kept)
        def _(h):
            for step in range(3):
                o_in[step, h] = jnp.zeros(o_in.shape[2:], o_in.dtype)
                l_in[step, h] = jnp.full(l_in.shape[2:], EXCLUDED, l_in.dtype)

    for step in range(3):
        @pl.when(me <= step)
        def _():
            for j in range(heads - kept):
                k_in[step, j] = jnp.zeros(k_in.shape[2:], k_in.dtype)
                v_in[step, j] = jnp.zeros(v_in.shape[2:], v_in.dtype)

    pl.semaphore_wait(
        barrier, 1 + has_left.astype(jnp.int32) + has_right.astype(jnp.int32)
    )

    @pl.when(has_right)
    def _():
        for j in range(heads - kept):
            for which in range(2):
                send_kv(which, 0, j).start()

    @pl.when(has_left)
    def _():
        for h in range(min(LEAD, kept)):
            send_q(0, h).start()

    @pl.loop(0, heads)
    def _(h):
        for which in range(3):
            load(which, h).start()

    def rounds(skew):
        return skew[0] + lax.rem(me, 2) * (skew[1] - skew[0])

    def staged(r, skew, distance, run):
        h = r - rounds(skew)
        @pl.when((h >= 0) & (h < kept) & (me + distance < n))
        def _():
            run(h)

    def staged_shipped(r, skew, run):
        j = r - rounds(skew)
        @pl.when((j >= 0) & (j < heads - kept))
        def _():
            run(j)

    def ship(step, j):
        @pl.when(me >= step)
        def _():
            for which in range(2):
                send_kv(which, step - 1, j).wait_recv()

                @pl.when(has_right)
                def _():
                    send_kv(which, step, j).start()

    def attend_shipped(j):
        h = kept + j
        for which in range(3):
            load(which, h).wait()

        @pl.when(me >= 3)
        def _():
            for which in range(2):
                send_kv(which, 2, j).wait_recv()

        ones = jnp.ones((rows, HEAD_DIM), jnp.bfloat16)
        for at in range(0, rows, tile):
            span = slice(at, at + tile)
            queries = q_own[h, span]
            parts = [causal(across(queries, k_own[h, : at + tile]), at)]
            for step in range(3):
                scores = across(queries, k_in[step, j])
                parts.append(jnp.where(me > step, scores, EXCLUDED))
            top = functools.reduce(
                jnp.maximum, [jnp.max(part, axis=1, keepdims=True) for part in parts]
            )
            both = jnp.zeros((tile, 2 * HEAD_DIM), jnp.float32)
            for step, scores in enumerate(parts):
                weights = jnp.exp2(scores * SCALE - top * SCALE).astype(jnp.bfloat16)
                values = v_in[step - 1, j] if step else v_own[h, : at + tile]
                values = jnp.concatenate([values, ones[: values.shape[0]]], 1)
                both += jnp.dot(weights, values, preferred_element_type=jnp.float32)
            mixed = both[:, :HEAD_DIM] / both[:, HEAD_DIM:]
            attended[h, span] = mixed
            squares[span] += mixed * mixed

    def causal(scores, at):
        target = lax.broadcasted_iota(jnp.int32, scores.shape, 0) + at
        source = lax.broadcasted_iota(jnp.int32, scores.shape, 1)
        return jnp.where(source <= target, scores, EXCLUDED)

    def forward(step, h):
        send_q(step - 1, h).wait_recv()

        @pl.when(has_left)
        def _():
            send_q(step, h).start()

    def attend(h):
        for which in range(3):
            load(which, h).wait()

        @pl.when(me + 3 < n)
        def _():
            send_q(2, h).wait_recv()

        slot = lax.rem(h, SLOTS)
        keys = k_own[h]
        values = jnp.concatenate([v_own[h], jnp.ones((rows, HEAD_DIM), jnp.bfloat16)], 1)
        lane = lax.broadcasted_iota(jnp.int32, (tile, HEAD_DIM), 1)
        for at in range(0, rows, tile):
            span = slice(at, at + tile)
            levels = jnp.zeros((tile, HEAD_DIM), jnp.float32)
            for distance in (3, 2, 1, 0):
                depth = rows if distance else at + tile
                queries = q_in[distance - 1, h, span] if distance else q_own[h, span]
                scores = across(queries, keys[:depth])
                if not distance:
                    scores = causal(scores, at)
                top = jnp.max(scores, axis=1, keepdims=True) * SCALE
                weights = jnp.exp2(scores * SCALE - top).astype(jnp.bfloat16)
                both = jnp.dot(weights, values[:depth], preferred_element_type=jnp.float32)
                total = both[:, HEAD_DIM:]
                output = both[:, :HEAD_DIM] * (1.0 / total)
                levels = jnp.where(lane == distance, top + jnp.log2(total), levels)
                if distance == 3:
                    o_out[0, h, span] = output.astype(jnp.bfloat16)
                else:
                    o_own[slot, distance, span] = output
            turned = levels.T
            l_out[0, h, :, span] = turned[3:4]
            l_own[slot, :, span] = turned[:4]

        @pl.when(me + 3 < n)
        def _():
            send_o(0, h).start()
            send_l(0, h).start()

    def merge(distance, h):
        step = 3 - distance

        @pl.when(has_left)
        def _():
            send_o(step - 1, h).wait_recv()
            send_l(step - 1, h).wait_recv()

        slot = lax.rem(h, SLOTS)
        here, before = l_own[slot, distance : distance + 1], l_in[step - 1, h]
        share = 1.0 / (1.0 + jnp.exp2(here - before))
        if distance:
            gap = -jnp.abs(here - before)
            l_out[step, h] = jnp.maximum(here, before) + jnp.log2(1.0 + jnp.exp2(gap))
        share = row_to_lanes(share)
        mine = o_own[slot, distance]
        mixed = mine + share * (o_in[step - 1, h].astype(jnp.float32) - mine)
        if distance:
            o_out[step, h] = mixed.astype(jnp.bfloat16)
            send_o(step, h).start()
            send_l(step, h).start()
        else:
            attended[h] = mixed
            squares[...] += mixed * mixed

    @pl.loop(0, kept + max(MERGE_0))
    def _(r):
        staged_shipped(r, SHIP_1, functools.partial(ship, 1))
        staged_shipped(r, SHIP_2, functools.partial(ship, 2))
        staged_shipped(r, ATTEND_SHIPPED, attend_shipped)
        staged(r, FORWARD_1, 1, functools.partial(forward, 1))
        staged(r, MERGE_2, 2, functools.partial(merge, 2))
        staged(r, ATTEND, 0, attend)

        @pl.when(has_left & (r + LEAD < kept))
        def _():
            send_q(0, r + LEAD).start()

        staged(r, MERGE_0, 0, functools.partial(merge, 0))
        staged(r, FORWARD_2, 2, functools.partial(forward, 2))
        staged(r, MERGE_1, 1, functools.partial(merge, 1))

    row_out[...] = lanes_to_row(
        jnp.broadcast_to(jnp.sum(squares[...], axis=1, keepdims=True), squares.shape)
    )
    send_s().start()

    def drain(buffer, sem):
        pltpu.make_async_copy(buffer, buffer, sem).wait()

    for step in range(3):
        @pl.when(has_left & (me + step < n))
        def _():
            drain(q_in.at[step], q_send.at[step])

        @pl.when(me + 3 - step < n)
        def _():
            drain(o_out.at[step], o_send.at[step])
            drain(l_out.at[step], l_send.at[step])

        @pl.when(has_right & (me >= step))
        def _():
            drain(k_in.at[step], kv_send.at[0, step])
            drain(v_in.at[step], kv_send.at[1, step])

    send_s().wait()
    scale_ref[...] = row_to_lanes(lax.rsqrt((row_out[...] + row_in[...]) / D + 1e-06))


def finish(gain_ref, attended, scale_ref, out_hbm, finished, sem):
    heads, rows, _ = attended.shape
    chunk = rows // 4

    def store(i):
        span = pl.ds(i * chunk, chunk)
        return pltpu.make_async_copy(finished.at[span], out_hbm.at[span], sem.at[i])

    for i in range(4):
        span = slice(i * chunk, (i + 1) * chunk)
        for h in range(heads):
            columns = slice(h * HEAD_DIM, (h + 1) * HEAD_DIM)
            scaled = attended[h, span] * scale_ref[span] * gain_ref[h]
            finished[span, columns] = scaled.astype(jnp.bfloat16)
        store(i).start()
    for i in range(4):
        store(i).wait()


def solution(mesh):
    n = mesh.shape["seq"]

    def shards(norm_gain, queries, keys, values):
        rows, width = queries.shape
        heads = width // HEAD_DIM
        kept = heads - SHIPPED
        by_head = (heads, rows, HEAD_DIM)
        moved = (3, kept, rows, HEAD_DIM)
        shipped = (3, SHIPPED, rows, HEAD_DIM)
        dma = pltpu.SemaphoreType.DMA
        gain = norm_gain.reshape(heads, 1, HEAD_DIM)
        whole = pl.BlockSpec(memory_space=pltpu.VMEM)
        attended, scale = pl.pallas_call(
            functools.partial(kernel, n, heads, kept, rows),
            out_shape=[
                pltpu.VMEM(by_head, jnp.float32),
                pltpu.VMEM((rows, HEAD_DIM), jnp.float32),
            ],
            in_specs=[pl.BlockSpec(memory_space=pl.ANY)] * 3,
            out_specs=[whole, whole],
            scratch_shapes=[
                pltpu.VMEM(by_head, jnp.bfloat16),
                pltpu.VMEM(by_head, jnp.bfloat16),
                pltpu.VMEM(by_head, jnp.bfloat16),
                pltpu.VMEM(moved, jnp.bfloat16),
                pltpu.VMEM(moved, jnp.bfloat16),
                pltpu.VMEM((3, kept, 1, rows), jnp.float32),
                pltpu.VMEM(moved, jnp.bfloat16),
                pltpu.VMEM((3, kept, 1, rows), jnp.float32),
                pltpu.VMEM((SLOTS, 3, rows, HEAD_DIM), jnp.float32),
                pltpu.VMEM((SLOTS, 4, rows), jnp.float32),
                pltpu.VMEM(shipped, jnp.bfloat16),
                pltpu.VMEM(shipped, jnp.bfloat16),
                pltpu.VMEM((rows, HEAD_DIM), jnp.float32),
                pltpu.VMEM((1, rows), jnp.float32),
                pltpu.VMEM((1, rows), jnp.float32),
                dma((3, heads)),
                dma((3,)),
                dma((3, kept)),
                dma((3,)),
                dma((3, kept)),
                dma((3,)),
                dma((3, kept)),
                dma((2, 3)),
                dma((2, 3, SHIPPED)),
                dma,
                dma,
            ],
            compiler_params=pltpu.CompilerParams(
                collective_id=0, has_side_effects=True, vmem_limit_bytes=56 << 20
            ),
            cost_estimate=pl.CostEstimate(
                flops=16 * heads * rows * rows * HEAD_DIM,
                bytes_accessed=8 * rows * width,
                transcendentals=4 * heads * rows * rows,
            ),
        )(queries, keys, values)
        return pl.pallas_call(
            finish,
            out_shape=jax.ShapeDtypeStruct(queries.shape, jnp.bfloat16),
            in_specs=[whole] * 3,
            out_specs=pl.BlockSpec(memory_space=pl.ANY),
            scratch_shapes=[pltpu.VMEM((rows, width), jnp.bfloat16), dma((4,))],
            compiler_params=pltpu.CompilerParams(vmem_limit_bytes=16 << 20),
        )(gain, attended, scale)

    placed = (P("mp"), P("seq", "mp"), P("seq", "mp"), P("seq", "mp"))
    return jax.shard_map(
        shards, mesh=mesh, in_specs=placed, out_specs=P("seq", "mp"), check_vma=False
    )
```

```python
import functools
import math

import jax
import jax.numpy as jnp
from jax import lax
from jax.experimental import pallas as pl
from jax.experimental.pallas import tpu as pltpu
from jax.sharding import PartitionSpec as P

D = 4096
HEAD_DIM = 128
MESH = pl.DeviceIdType.MESH
SCALE = math.log2(math.e) / math.sqrt(HEAD_DIM)
EXCLUDED = -1e30

SHIPPED = 2
LEAD = 2
FORWARD_1, FORWARD_2, ATTEND, MERGE_2, MERGE_1, MERGE_0 = (1, 3), (1, 5), (4, 6), (6, 7), (7, 8), (10, 12)
SHIP_1, SHIP_2, ATTEND_SHIPPED = (2, 2), (4, 5), (6, 7)
SLOTS = max(b - a for a, b in zip(ATTEND, MERGE_0)) + 1
TILE = 128


def across(a, b):
    return lax.dot_general(a, b, (((1,), (1,)), ((), ())), preferred_element_type=jnp.float32)


def lanes_to_row(column):
    return column.T[:1]


def row_to_lanes(row):
    return jnp.broadcast_to(row, (HEAD_DIM, row.shape[1])).T


def kernel(
    n, heads, kept, rows,
    q_hbm, k_hbm, v_hbm, attended, scale_ref,
    q_own, k_own, v_own, q_in, o_in, l_in, o_out, l_out, o_own, l_own, k_in, v_in,
    squares, row_out, row_in,
    load_sem, q_send, q_recv, o_send, o_recv, l_send, l_recv, kv_send, kv_recv, s_send, s_recv,
):
    me = lax.axis_index("seq")
    partner = 1 - lax.axis_index("mp")
    left, right = jnp.maximum(me - 1, 0), jnp.minimum(me + 1, n - 1)
    has_left, has_right = me > 0, me < n - 1
    tile = min(TILE, rows)
    to_left, to_right = {"seq": left}, {"seq": right}

    def columns(h):
        return pl.ds(pl.multiple_of(h * HEAD_DIM, HEAD_DIM), HEAD_DIM)

    def load(which, h):
        source, target = ((q_hbm, q_own), (k_hbm, k_own), (v_hbm, v_own))[which]
        return pltpu.make_async_copy(
            source.at[:, columns(h)], target.at[h], load_sem.at[which, h]
        )

    def send_q(step, h):
        source = q_hbm.at[:, columns(h)] if step == 0 else q_in.at[step - 1, h]
        return pltpu.make_async_remote_copy(
            src_ref=source, dst_ref=q_in.at[step, h],
            send_sem=q_send.at[step], recv_sem=q_recv.at[step, h],
            device_id=to_left, device_id_type=MESH,
        )

    def send_o(step, h):
        return pltpu.make_async_remote_copy(
            src_ref=o_out.at[step, h], dst_ref=o_in.at[step, h],
            send_sem=o_send.at[step], recv_sem=o_recv.at[step, h],
            device_id=to_right, device_id_type=MESH,
        )

    def send_l(step, h):
        return pltpu.make_async_remote_copy(
            src_ref=l_out.at[step, h], dst_ref=l_in.at[step, h],
            send_sem=l_send.at[step], recv_sem=l_recv.at[step, h],
            device_id=to_right, device_id_type=MESH,
        )

    def send_kv(which, step, j):
        source, target = ((k_hbm, k_in), (v_hbm, v_in))[which]
        source = target.at[step - 1, j] if step else source.at[:, columns(kept + j)]
        return pltpu.make_async_remote_copy(
            src_ref=source, dst_ref=target.at[step, j],
            send_sem=kv_send.at[which, step], recv_sem=kv_recv.at[which, step, j],
            device_id=to_right, device_id_type=MESH,
        )

    def send_s():
        return pltpu.make_async_remote_copy(
            src_ref=row_out, dst_ref=row_in, send_sem=s_send, recv_sem=s_recv,
            device_id={"mp": partner}, device_id_type=MESH,
        )

    barrier = pltpu.get_barrier_semaphore()

    @pl.when(has_left)
    def _():
        pl.semaphore_signal(barrier, inc=1, device_id=to_left, device_id_type=MESH)

    @pl.when(has_right)
    def _():
        pl.semaphore_signal(barrier, inc=1, device_id=to_right, device_id_type=MESH)

    pl.semaphore_signal(barrier, inc=1, device_id={"mp": partner}, device_id_type=MESH)

    @pl.loop(0, heads)
    def _(h):
        for which in range(3):
            load(which, h).start()

    squares[...] = jnp.zeros_like(squares)

    @pl.when(jnp.logical_not(has_left))
    def _():
        @pl.loop(0, kept)
        def _(h):
            for step in range(3):
                o_in[step, h] = jnp.zeros(o_in.shape[2:], o_in.dtype)
                l_in[step, h] = jnp.full(l_in.shape[2:], EXCLUDED, l_in.dtype)

    for step in range(3):
        @pl.when(me <= step)
        def _():
            for j in range(heads - kept):
                k_in[step, j] = jnp.zeros(k_in.shape[2:], k_in.dtype)
                v_in[step, j] = jnp.zeros(v_in.shape[2:], v_in.dtype)

    pl.semaphore_wait(
        barrier, 1 + has_left.astype(jnp.int32) + has_right.astype(jnp.int32)
    )

    @pl.when(has_right)
    def _():
        for j in range(heads - kept):
            for which in range(2):
                send_kv(which, 0, j).start()

    @pl.when(has_left)
    def _():
        for h in range(min(LEAD, kept)):
            send_q(0, h).start()

    def rounds(skew):
        return skew[0] + lax.rem(me, 2) * (skew[1] - skew[0])

    def staged(r, skew, distance, run):
        h = r - rounds(skew)
        @pl.when((h >= 0) & (h < kept) & (me + distance < n))
        def _():
            run(h)

    def staged_shipped(r, skew, run):
        j = r - rounds(skew)
        @pl.when((j >= 0) & (j < heads - kept))
        def _():
            run(j)

    def ship(step, j):
        @pl.when(me >= step)
        def _():
            for which in range(2):
                send_kv(which, step - 1, j).wait_recv()

                @pl.when(has_right)
                def _():
                    send_kv(which, step, j).start()

    def attend_shipped(j):
        h = kept + j
        for which in range(3):
            load(which, h).wait()

        @pl.when(me >= 3)
        def _():
            for which in range(2):
                send_kv(which, 2, j).wait_recv()

        ones = jnp.ones((rows, HEAD_DIM), jnp.bfloat16)
        for at in range(0, rows, tile):
            span = slice(at, at + tile)
            queries = q_own[h, span]
            parts = [causal(across(queries, k_own[h, : at + tile]), at)]
            for step in range(3):
                scores = across(queries, k_in[step, j])
                parts.append(jnp.where(me > step, scores, EXCLUDED))
            top = functools.reduce(
                jnp.maximum, [jnp.max(part, axis=1, keepdims=True) for part in parts]
            )
            both = jnp.zeros((tile, 2 * HEAD_DIM), jnp.float32)
            for step, scores in enumerate(parts):
                weights = jnp.exp2(scores * SCALE - top * SCALE).astype(jnp.bfloat16)
                values = v_in[step - 1, j] if step else v_own[h, : at + tile]
                values = jnp.concatenate([values, ones[: values.shape[0]]], 1)
                both += jnp.dot(weights, values, preferred_element_type=jnp.float32)
            mixed = both[:, :HEAD_DIM] / both[:, HEAD_DIM:]
            attended[h, span] = mixed
            squares[span] += mixed * mixed

    def causal(scores, at):
        target = lax.broadcasted_iota(jnp.int32, scores.shape, 0) + at
        source = lax.broadcasted_iota(jnp.int32, scores.shape, 1)
        return jnp.where(source <= target, scores, EXCLUDED)

    def forward(step, h):
        send_q(step - 1, h).wait_recv()

        @pl.when(has_left)
        def _():
            send_q(step, h).start()

    def attend(h):
        for which in range(3):
            load(which, h).wait()

        @pl.when(me + 3 < n)
        def _():
            send_q(2, h).wait_recv()

        slot = lax.rem(h, SLOTS)
        keys = k_own[h]
        values = jnp.concatenate([v_own[h], jnp.ones((rows, HEAD_DIM), jnp.bfloat16)], 1)
        lane = lax.broadcasted_iota(jnp.int32, (tile, HEAD_DIM), 1)
        for at in range(0, rows, tile):
            span = slice(at, at + tile)
            levels = jnp.zeros((tile, HEAD_DIM), jnp.float32)
            for distance in (3, 2, 1, 0):
                depth = rows if distance else at + tile
                queries = q_in[distance - 1, h, span] if distance else q_own[h, span]
                scores = across(queries, keys[:depth])
                if not distance:
                    scores = causal(scores, at)
                top = jnp.max(scores, axis=1, keepdims=True) * SCALE
                weights = jnp.exp2(scores * SCALE - top).astype(jnp.bfloat16)
                both = jnp.dot(weights, values[:depth], preferred_element_type=jnp.float32)
                total = both[:, HEAD_DIM:]
                output = both[:, :HEAD_DIM] * (1.0 / total)
                levels = jnp.where(lane == distance, top + jnp.log2(total), levels)
                if distance == 3:
                    o_out[0, h, span] = output.astype(jnp.bfloat16)
                else:
                    o_own[slot, distance, span] = output
            turned = levels.T
            l_out[0, h, :, span] = turned[3:4]
            l_own[slot, :, span] = turned[:4]

        @pl.when(me + 3 < n)
        def _():
            send_l(0, h).start()
            send_o(0, h).start()

    def merge(distance, h):
        step = 3 - distance

        @pl.when(has_left)
        def _():
            send_l(step - 1, h).wait_recv()

        slot = lax.rem(h, SLOTS)
        here, before = l_own[slot, distance : distance + 1], l_in[step - 1, h]
        share = 1.0 / (1.0 + jnp.exp2(here - before))
        if distance:
            gap = -jnp.abs(here - before)
            l_out[step, h] = jnp.maximum(here, before) + jnp.log2(1.0 + jnp.exp2(gap))
            send_l(step, h).start()
        share = row_to_lanes(share)

        @pl.when(has_left)
        def _():
            send_o(step - 1, h).wait_recv()

        mine = o_own[slot, distance]
        mixed = mine + share * (o_in[step - 1, h].astype(jnp.float32) - mine)
        if distance:
            o_out[step, h] = mixed.astype(jnp.bfloat16)
            send_o(step, h).start()
        else:
            attended[h] = mixed
            squares[...] += mixed * mixed

    @pl.loop(0, kept + max(MERGE_0))
    def _(r):
        staged_shipped(r, SHIP_1, functools.partial(ship, 1))
        staged_shipped(r, SHIP_2, functools.partial(ship, 2))
        staged_shipped(r, ATTEND_SHIPPED, attend_shipped)
        staged(r, FORWARD_1, 1, functools.partial(forward, 1))
        staged(r, MERGE_0, 0, functools.partial(merge, 0))

        @pl.when(has_left & (r + LEAD < kept))
        def _():
            send_q(0, r + LEAD).start()

        staged(r, MERGE_2, 2, functools.partial(merge, 2))
        staged(r, ATTEND, 0, attend)
        staged(r, FORWARD_2, 2, functools.partial(forward, 2))
        staged(r, MERGE_1, 1, functools.partial(merge, 1))

    row_out[...] = lanes_to_row(
        jnp.broadcast_to(jnp.sum(squares[...], axis=1, keepdims=True), squares.shape)
    )
    send_s().start()

    def drain(buffer, sem):
        pltpu.make_async_copy(buffer, buffer, sem).wait()

    for step in range(3):
        @pl.when(has_left & (me + step < n))
        def _():
            drain(q_in.at[step], q_send.at[step])

        @pl.when(me + 3 - step < n)
        def _():
            drain(o_out.at[step], o_send.at[step])
            drain(l_out.at[step], l_send.at[step])

        @pl.when(has_right & (me >= step))
        def _():
            drain(k_in.at[step], kv_send.at[0, step])
            drain(v_in.at[step], kv_send.at[1, step])

    send_s().wait()
    scale_ref[...] = row_to_lanes(lax.rsqrt((row_out[...] + row_in[...]) / D + 1e-06))


def finish(gain_ref, attended, scale_ref, out_hbm, finished, sem):
    heads, rows, _ = attended.shape
    chunk = rows // 4

    def store(i):
        span = pl.ds(i * chunk, chunk)
        return pltpu.make_async_copy(finished.at[span], out_hbm.at[span], sem.at[i])

    for i in range(4):
        span = slice(i * chunk, (i + 1) * chunk)
        for h in range(heads):
            columns = slice(h * HEAD_DIM, (h + 1) * HEAD_DIM)
            scaled = attended[h, span] * scale_ref[span] * gain_ref[h]
            finished[span, columns] = scaled.astype(jnp.bfloat16)
        store(i).start()
    for i in range(4):
        store(i).wait()


def solution(mesh):
    n = mesh.shape["seq"]

    def shards(norm_gain, queries, keys, values):
        rows, width = queries.shape
        heads = width // HEAD_DIM
        kept = heads - SHIPPED
        by_head = (heads, rows, HEAD_DIM)
        moved = (3, kept, rows, HEAD_DIM)
        shipped = (3, SHIPPED, rows, HEAD_DIM)
        dma = pltpu.SemaphoreType.DMA
        gain = norm_gain.reshape(heads, 1, HEAD_DIM)
        whole = pl.BlockSpec(memory_space=pltpu.VMEM)
        attended, scale = pl.pallas_call(
            functools.partial(kernel, n, heads, kept, rows),
            out_shape=[
                pltpu.VMEM(by_head, jnp.float32),
                pltpu.VMEM((rows, HEAD_DIM), jnp.float32),
            ],
            in_specs=[pl.BlockSpec(memory_space=pl.ANY)] * 3,
            out_specs=[whole, whole],
            scratch_shapes=[
                pltpu.VMEM(by_head, jnp.bfloat16),
                pltpu.VMEM(by_head, jnp.bfloat16),
                pltpu.VMEM(by_head, jnp.bfloat16),
                pltpu.VMEM(moved, jnp.bfloat16),
                pltpu.VMEM(moved, jnp.bfloat16),
                pltpu.VMEM((3, kept, 1, rows), jnp.float32),
                pltpu.VMEM(moved, jnp.bfloat16),
                pltpu.VMEM((3, kept, 1, rows), jnp.float32),
                pltpu.VMEM((SLOTS, 3, rows, HEAD_DIM), jnp.float32),
                pltpu.VMEM((SLOTS, 4, rows), jnp.float32),
                pltpu.VMEM(shipped, jnp.bfloat16),
                pltpu.VMEM(shipped, jnp.bfloat16),
                pltpu.VMEM((rows, HEAD_DIM), jnp.float32),
                pltpu.VMEM((1, rows), jnp.float32),
                pltpu.VMEM((1, rows), jnp.float32),
                dma((3, heads)),
                dma((3,)),
                dma((3, kept)),
                dma((3,)),
                dma((3, kept)),
                dma((3,)),
                dma((3, kept)),
                dma((2, 3)),
                dma((2, 3, SHIPPED)),
                dma,
                dma,
            ],
            compiler_params=pltpu.CompilerParams(
                collective_id=0, has_side_effects=True, vmem_limit_bytes=56 << 20
            ),
            cost_estimate=pl.CostEstimate(
                flops=16 * heads * rows * rows * HEAD_DIM,
                bytes_accessed=8 * rows * width,
                transcendentals=4 * heads * rows * rows,
            ),
        )(queries, keys, values)
        return pl.pallas_call(
            finish,
            out_shape=jax.ShapeDtypeStruct(queries.shape, jnp.bfloat16),
            in_specs=[whole] * 3,
            out_specs=pl.BlockSpec(memory_space=pl.ANY),
            scratch_shapes=[pltpu.VMEM((rows, width), jnp.bfloat16), dma((4,))],
            compiler_params=pltpu.CompilerParams(vmem_limit_bytes=16 << 20),
        )(gain, attended, scale)

    placed = (P("mp"), P("seq", "mp"), P("seq", "mp"), P("seq", "mp"))
    return jax.shard_map(
        shards, mesh=mesh, in_specs=placed, out_specs=P("seq", "mp"), check_vma=False
    )
```
